32 devices in a mesh: dp: 8 (over z, x), tensor: 4 (over y, core).
Axes of the slice: x: 2, y: 2, z: 4, core: 2. Of those that a mesh axis runs over, the one named last changes fastest.
Arguments:
- grads: bfloat16 [8, 3072, 8192], P('dp', None, 'tensor'), may hold values from -8 to 8
- errors: bfloat16 [8, 3072, 8192], P('dp', None, 'tensor'), may hold values from -4 to 4
- q_init: float32 [8192, 32], P('tensor'), may hold values from -0.0625 to 0.0625
Outputs:
- left_sum: float32 [3072, 32], P(('dp', 'tensor'))
- right: float32 [8192, 32], P('tensor')
- new_errors: bfloat16 [8, 3072, 8192], P('dp', None, 'tensor')
The draws below stay inside these ranges and needn't reach their ends.
All inputs are finite; a program needn't handle non-finite values.
Results may differ from the reference program's by a relative error of at most 0.0085.
Values sent between devices are 32-bit elements; how exact they have to be, the bound alone decides.
A program may use at most 128 MiB of HBM per device.

```python
import jax
import jax.numpy as jnp
from jax import lax

D = 3072
FF = 8192
R = 32
REPLICAS = 8


def draw_grads(key, part):
    key = jax.random.fold_in(key, 11)
    first, second = jax.random.split(key, 2)
    common = jax.random.normal(first, (D, FF), jnp.float32)
    noise = jax.random.normal(second, (REPLICAS, D, FF), jnp.float32)
    values = 0.7 * common + 0.7 * noise
    return jnp.clip(values, -8.0, 8.0).astype(jnp.bfloat16)


def level_of(own_key, dims, cuts, least, largest):
    level, own = 1.0, jax.random.fold_in(own_key, 6)
    for position, parts in cuts:
        steps = jnp.exp(jax.random.uniform(jax.random.fold_in(own, position), (parts,), jnp.float32, least / len(cuts), largest / len(cuts)))
        level = level * jnp.repeat(steps, dims[position] // parts).reshape([-1 if axis == position else 1 for axis in range(len(dims))])
    return level


def centred(own_key, shape, spread, bound, cuts=(), kind=jnp.bfloat16):
    array = spread * jax.random.normal(own_key, shape, jnp.float32)
    if cuts:
        array = array * level_of(own_key, shape, cuts, -0.22, 0.18)
    return jnp.clip(array, -bound, bound).astype(kind)


def setup_inputs(seed: int = 0) -> dict:
    key_of = jax.random.split(jax.random.key(seed), 4)
    return {
        "grads": draw_grads(jax.random.fold_in(key_of[3], 71), 0),
        "errors": centred(key_of[1], (REPLICAS, D, FF), 0.5, 4.0, ((0, 8), (2, 4))),
        "q_init": centred(key_of[2], (FF, R), FF ** -0.5, 0.0625, ((0, 4),), jnp.float32),
    }


def reference(grads, errors, q_init):
    q_low = q_init.astype(jnp.bfloat16)

    def left_term(pair):
        merged = (pair[0].astype(jnp.float32) + pair[1].astype(jnp.float32)).astype(jnp.bfloat16)
        return jnp.dot(merged.astype(jnp.float32), q_low.astype(jnp.float32), preferred_element_type=jnp.float32)
    left_sum = jnp.sum(lax.map(left_term, (grads, errors)), axis=0) / REPLICAS
    gram = jnp.dot(left_sum.T, left_sum, precision=lax.Precision.HIGHEST)
    lower = jnp.linalg.cholesky(gram)
    basis = jax.scipy.linalg.solve_triangular(lower, left_sum.T, lower=True).T
    basis_low = basis.astype(jnp.bfloat16)

    def right_term(pair):
        merged = (pair[0].astype(jnp.float32) + pair[1].astype(jnp.float32)).astype(jnp.bfloat16)
        return jnp.dot(merged.T.astype(jnp.float32), basis_low.astype(jnp.float32), preferred_element_type=jnp.float32)
    right = jnp.sum(lax.map(right_term, (grads, errors)), axis=0) / REPLICAS
    approx = jnp.dot(basis, right.T, precision=lax.Precision.HIGHEST)

    def renew(pair):
        merged = (pair[0].astype(jnp.float32) + pair[1].astype(jnp.float32)).astype(jnp.bfloat16)
        return (merged.astype(jnp.float32) - approx).astype(jnp.bfloat16)
    new_errors = lax.map(renew, (grads, errors))
    return (left_sum, right, new_errors)
```

```python
import functools

import jax
import jax.numpy as jnp
from jax import lax
from jax.experimental import pallas as pl
from jax.experimental.pallas import tpu as pltpu
from jax.sharding import PartitionSpec as P

MESH = pl.DeviceIdType.MESH
NT = (((1,), (1,)), ((), ()))
TN = (((0,), (0,)), ((), ()))
BF16, F32 = jnp.bfloat16, jnp.float32
CHUNKS = 3
SLOTS = 4


def split(x):
    high = x.astype(BF16)
    return high, (x - high.astype(F32)).astype(BF16)


def inverse_factor(gram, rank):
    rows = lax.broadcasted_iota(jnp.int32, (rank, 128), 0)
    lanes = lax.broadcasted_iota(jnp.int32, (rank, 128), 1)
    eye = jnp.where(lanes == rows + rank, 1.0, 0.0).astype(F32)
    pad = jnp.concatenate([gram, jnp.zeros((rank, 128 - rank), F32)], axis=1)
    work = pad + eye
    scale = jnp.zeros((rank, 128), F32)
    for j in range(rank):
        row = work[j:j + 1, :]
        pivot = row[:, j:j + 1]
        column = work[:, j:j + 1]
        scale = jnp.where(rows == j, lax.rsqrt(pivot), scale)
        factor = jnp.where(rows[:, :1] > j, column / pivot, 0.0)
        work = work - factor * row
    return (work * scale)[:, rank:2 * rank]


def exchange(T, N, rank, g_hbm, e_hbm, q_ref, merged_ref, left_ref, basis_ref, right_ref,
             gbuf, ebuf, part, s1r, s2s, s2r, full, acc, s5s, s5r, total,
             gsem, esem, s1a, s1b, s2a, s2b, s3a, s3b, s4a, s4b, s5a, s5b, s6a, s6b):
    t, p = lax.axis_index("tensor"), lax.axis_index("dp")
    depth, width = merged_ref.shape
    rows = depth // (CHUNKS * T)
    tiles = CHUNKS * T
    owners, groups, halves = s2s.shape[1], rank // 8, rows // 128
    columns = acc.shape[2]
    blocks = width // columns
    per = N // blocks

    def load(i):
        slot = lax.rem(i, SLOTS)
        where = pl.ds(pl.multiple_of(i * rows, rows), rows)
        return (pltpu.make_async_copy(g_hbm.at[where], gbuf.at[slot], gsem.at[slot]),
                pltpu.make_async_copy(e_hbm.at[where], ebuf.at[slot], esem.at[slot]))

    for i in range(SLOTS):
        for copy in load(i):
            copy.start()

    barrier = pltpu.get_barrier_semaphore()
    for k in range(1, T):
        pl.semaphore_signal(barrier, inc=1, device_id={"tensor": lax.rem(t + k, T)}, device_id_type=MESH)
    for k in range(1, N):
        pl.semaphore_signal(barrier, inc=1, device_id={"dp": lax.rem(p + k, N)}, device_id_type=MESH)
    q_low = q_ref[...].astype(BF16)
    waited = T + N - 2

    def send(src, dst, a, b, axis, peer):
        return pltpu.make_async_remote_copy(
            src_ref=src, dst_ref=dst, send_sem=a, recv_sem=b,
            device_id={axis: peer}, device_id_type=MESH)

    def to_tensor(k):
        return lax.rem(t + k, T)

    def to_dp(k):
        return lax.rem(p + k, N)

    def from_dp(k):
        return lax.rem(p + (N - k), N)

    def when_owner(index, body):
        if owners == N:
            body()
        else:
            pl.when(index < owners)(body)

    def compute(c):
        def tile(i, carry):
            g, e = load(i)
            g.wait()
            e.wait()
            slot = lax.rem(i, SLOTS)
            merged = (gbuf[slot].astype(F32) + ebuf[slot].astype(F32)).astype(BF16)
            merged_ref[pl.ds(pl.multiple_of(i * rows, rows), rows), :] = merged
            part[i] = lax.dot_general(q_low, merged, NT, preferred_element_type=F32)

            @pl.when(i + SLOTS < tiles)
            def _():
                for copy in load(i + SLOTS):
                    copy.start()
            return carry
        lax.fori_loop(c * T, (c + 1) * T, tile, 0)

    def copy1(c, k):
        return send(part.at[c * T + to_tensor(k)], s1r.at[c, k - 1], s1a.at[c, k - 1], s1b.at[c, k - 1], "tensor", to_tensor(k))

    def stage1(c):
        for k in range(1, T):
            copy1(c, k).start()

    def copy2(c, k):
        piece = to_dp(k) if owners == N else jnp.minimum(to_dp(k), owners - 1)
        return send(s2s.at[c, piece], s2r.at[c, k - 1], s2a.at[c, k - 1], s2b.at[c, k - 1], "dp", to_dp(k))

    def stage2(c):
        value = part[c * T + t]
        for k in range(1, T):
            copy1(c, k).wait_recv()
            value = value + s1r[c, k - 1]
        value = value * (1.0 / N)
        for h in range(halves):
            for g in range(groups):
                s2s[c, h * groups + g] = value[g * 8:(g + 1) * 8, h * 128:(h + 1) * 128]
        for k in range(1, N):
            when_owner(to_dp(k), lambda k=k: copy2(c, k).start())

    def copy3(c, k):
        piece = full.at[c, t, p if owners == N else jnp.minimum(p, owners - 1)]
        return send(piece, piece, s3a.at[c, k - 1], s3b.at[c, k - 1], "dp", to_dp(k))

    def stage3(c):
        def body():
            value = s2s[c, p]
            for k in range(1, N):
                copy2(c, k).wait_recv()
                value = value + s2r[c, k - 1]
            full[c, t, p] = value
            for k in range(1, N):
                copy3(c, k).start()
        when_owner(p, body)

    def copy4(c, k):
        return send(full.at[c, t], full.at[c, t], s4a.at[c, k - 1], s4b.at[c, k - 1], "tensor", to_tensor(k))

    def stage4(c):
        for k in range(1, N):
            when_owner(from_dp(k), lambda k=k: copy3(c, k).wait_recv())
        for k in range(1, T):
            copy4(c, k).start()

    def chunk_left(c):
        pieces = []
        for s in range(T):
            for h in range(halves):
                pieces.append(full[c, s, h * groups:(h + 1) * groups].reshape(rank, 128))
        return jnp.concatenate(pieces, axis=1)

    length = T * rows

    def copy5(k):
        return send(s5s.at[to_dp(k)], s5r.at[k - 1], s5a.at[k - 1], s5b.at[k - 1], "dp", to_dp(k))

    def stage5(c):
        for k in range(1, T):
            copy4(c, k).wait_recv()
        left = chunk_left(c)
        left_ref[:, c * length:(c + 1) * length] = left
        both = jnp.concatenate(split(left), axis=0)
        last = c == CHUNKS - 1

        def block(b):
            where = pl.ds(pl.multiple_of(b * columns, columns), columns)
            out = jnp.dot(both, merged_ref[c * length:(c + 1) * length, where], preferred_element_type=F32)
            out = out[:rank] + out[rank:]
            if c > 0:
                out = out + acc[b]
            if not last:
                acc[b] = out
            else:
                high = rank // per
                for i in range(per):
                    s5s[b * per + i] = out[i * high:(i + 1) * high] * (1.0 / N)

        if not last or per > 1:
            def step(b, carry):
                block(b)
                return carry
            lax.fori_loop(0, blocks, step, 0)
            if last:
                for k in range(1, N):
                    copy5(k).start()
        else:
            for k in range(1, N):
                block(to_dp(k))
                copy5(k).start()
            block(p)

    compute(0)
    pl.semaphore_wait(barrier, waited)
    stage1(0)
    compute(1)
    stage1(1)
    stage2(0)
    compute(2)
    stage1(2)
    stage2(1)
    stage3(0)
    stage2(2)
    stage3(1)
    stage4(0)
    stage3(2)
    stage4(1)
    stage5(0)
    stage4(2)
    stage5(1)
    stage5(2)

    left = left_ref[...]
    gram = lax.dot_general(left, left, NT, precision=lax.Precision.HIGHEST, preferred_element_type=F32)
    inverse = inverse_factor(gram, rank)

    def copy6(k):
        return send(total.at[p], total.at[p], s6a.at[k - 1], s6b.at[k - 1], "dp", to_dp(k))

    value = s5s[p]
    for k in range(1, N):
        copy5(k).wait_recv()
        value = value + s5r[k - 1]
    total[p] = value
    for k in range(1, N):
        copy6(k).start()
    basis = jnp.dot(inverse, left, precision=lax.Precision.HIGHEST, preferred_element_type=F32)
    high, low = split(basis)
    basis_ref[...] = jnp.concatenate([high, low, high], axis=0)
    for k in range(1, N):
        copy6(k).wait_recv()
    for b in range(blocks):
        value = jnp.concatenate([total[b * per + i] for i in range(per)], axis=0)
        right_ref[:, b * columns:(b + 1) * columns] = jnp.dot(
            inverse, value, precision=lax.Precision.HIGHEST, preferred_element_type=F32)

    for c in range(CHUNKS):
        for k in range(1, T):
            copy1(c, k).wait_send()
            copy4(c, k).wait_send()
        for k in range(1, N):
            when_owner(to_dp(k), lambda k=k: copy2(c, k).wait_send())
            when_owner(p, lambda k=k: copy3(c, k).wait_send())
    for k in range(1, N):
        copy5(k).wait_send()
        copy6(k).wait_send()


def renew(basis_ref, right_ref, merged_ref, new_ref, out_ref):
    i = pl.program_id(0)
    rows, width = new_ref.shape

    @pl.when(i == 0)
    def _():
        out_ref[...] = right_ref[...]

    start = pl.multiple_of(i * rows, rows)
    step = 512
    basis = basis_ref[...]
    for b in range(width // step):
        cut = slice(b * step, (b + 1) * step)
        high, low = split(right_ref[:, cut])
        factor = jnp.concatenate([high, high, low], axis=0)
        approx = lax.dot_general(basis, factor, TN, preferred_element_type=F32)
        new_ref[:, cut] = (merged_ref[pl.ds(start, rows), cut].astype(F32) - approx).astype(BF16)


def on_device(T, N, grads, errors, q_init):
    depth, width = grads.shape[1:]
    rank = q_init.shape[1]
    rows = depth // (CHUNKS * T)
    owners = (rank // 8) * (rows // 128)
    blocks = min(N, width // 128)
    per = N // blocks
    columns = width // blocks
    piece = (rank // per, columns)
    vmem = pl.BlockSpec(memory_space=pltpu.VMEM)
    hbm = pl.BlockSpec(memory_space=pl.ANY)
    dma = pltpu.SemaphoreType.DMA
    merged, left, basis, right = pl.pallas_call(
        functools.partial(exchange, T, N, rank),
        out_shape=(
            pltpu.VMEM((depth, width), BF16),
            jax.ShapeDtypeStruct((rank, depth), F32),
            jax.ShapeDtypeStruct((3 * rank, depth), BF16),
            jax.ShapeDtypeStruct((rank, width), F32),
        ),
        in_specs=[hbm, hbm, vmem],
        out_specs=(vmem, vmem, vmem, vmem),
        scratch_shapes=[
            pltpu.VMEM((SLOTS, rows, width), BF16),
            pltpu.VMEM((SLOTS, rows, width), BF16),
            pltpu.VMEM((CHUNKS * T, rank, rows), F32),
            pltpu.VMEM((CHUNKS, T - 1, rank, rows), F32),
            pltpu.VMEM((CHUNKS, owners, 8, 128), F32),
            pltpu.VMEM((CHUNKS, N - 1, 8, 128), F32),
            pltpu.VMEM((CHUNKS, T, owners, 8, 128), F32),
            pltpu.VMEM((blocks, rank, columns), F32),
            pltpu.VMEM((N,) + piece, F32),
            pltpu.VMEM((N - 1,) + piece, F32),
            pltpu.VMEM((N,) + piece, F32),
            dma((SLOTS,)), dma((SLOTS,)),
            dma((CHUNKS, T - 1)), dma((CHUNKS, T - 1)),
            dma((CHUNKS, N - 1)), dma((CHUNKS, N - 1)),
            dma((CHUNKS, N - 1)), dma((CHUNKS, N - 1)),
            dma((CHUNKS, T - 1)), dma((CHUNKS, T - 1)),
            dma((N - 1,)), dma((N - 1,)),
            dma((N - 1,)), dma((N - 1,)),
        ],
        compiler_params=pltpu.CompilerParams(
            collective_id=0, has_side_effects=True, vmem_limit_bytes=24 * 2 ** 20),
    )(grads[0], errors[0], q_init.T)

    renew_rows = 256
    renewed, right_out = pl.pallas_call(
        renew,
        grid=(depth // renew_rows,),
        out_shape=(jax.ShapeDtypeStruct((depth, width), BF16), jax.ShapeDtypeStruct((rank, width), F32)),
        in_specs=[
            pl.BlockSpec((3 * rank, renew_rows), lambda i: (0, i)),
            pl.BlockSpec((rank, width), lambda i: (0, 0)),
            vmem,
        ],
        out_specs=(
            pl.BlockSpec((renew_rows, width), lambda i: (i, 0)),
            pl.BlockSpec((rank, width), lambda i: (0, 0)),
        ),
        compiler_params=pltpu.CompilerParams(vmem_limit_bytes=16 * 2 ** 20),
    )(basis, right, merged)

    share = depth // (N * T)
    position = lax.axis_index(("dp", "tensor"))
    left_out = lax.dynamic_slice_in_dim(left, position * share, share, 1).T
    return (left_out, right_out.T, renewed[None])


def solution(mesh):
    return jax.shard_map(
        functools.partial(on_device, mesh.shape["tensor"], mesh.shape["dp"]),
        mesh=mesh,
        in_specs=(P("dp", None, "tensor"), P("dp", None, "tensor"), P("tensor", None)),
        out_specs=(P(("dp", "tensor"), None), P("tensor", None), P("dp", None, "tensor")),
        check_vma=False,
    )
```

```python
import functools

import jax
import jax.numpy as jnp
from jax import lax
from jax.experimental import pallas as pl
from jax.experimental.pallas import tpu as pltpu
from jax.sharding import PartitionSpec as P

MESH = pl.DeviceIdType.MESH
NT = (((1,), (1,)), ((), ()))
TN = (((0,), (0,)), ((), ()))
BF16, F32 = jnp.bfloat16, jnp.float32
CHUNKS = 3
SLOTS = 4


def split(x):
    high = x.astype(BF16)
    return high, (x - high.astype(F32)).astype(BF16)


def eliminate(state, rank, steps):
    work, scale = state
    rows = lax.broadcasted_iota(jnp.int32, (rank, 128), 0)
    for j in steps:
        row = work[j:j + 1, :]
        pivot = row[:, j:j + 1]
        column = work[:, j:j + 1]
        scale = jnp.where(rows == j, lax.rsqrt(pivot), scale)
        factor = jnp.where(rows[:, :1] > j, column / pivot, 0.0)
        work = work - factor * row
    return work, scale


def augmented(gram, rank):
    rows = lax.broadcasted_iota(jnp.int32, (rank, 128), 0)
    lanes = lax.broadcasted_iota(jnp.int32, (rank, 128), 1)
    eye = jnp.where(lanes == rows + rank, 1.0, 0.0).astype(F32)
    pad = jnp.concatenate([gram, jnp.zeros((rank, 128 - rank), F32)], axis=1)
    return pad + eye, jnp.zeros((rank, 128), F32)


def exchange(T, N, rank, g_hbm, e_hbm, q_ref, merged_ref, left_ref, basis_ref, right_ref,
             gbuf, ebuf, part, s1r, s2s, s2r, full, acc, s5s, s5r, total,
             gsem, esem, s1a, s1b, s2a, s2b, s3a, s3b, s4a, s4b, s5a, s5b, s6a, s6b):
    t, p = lax.axis_index("tensor"), lax.axis_index("dp")
    depth, width = merged_ref.shape
    rows = depth // (CHUNKS * T)
    tiles = CHUNKS * T
    owners, groups, halves = s2s.shape[1], rank // 8, rows // 128
    columns = acc.shape[2]
    blocks = width // columns
    per = N // blocks

    def load(i):
        slot = lax.rem(i, SLOTS)
        where = pl.ds(pl.multiple_of(i * rows, rows), rows)
        return (pltpu.make_async_copy(g_hbm.at[where], gbuf.at[slot], gsem.at[slot]),
                pltpu.make_async_copy(e_hbm.at[where], ebuf.at[slot], esem.at[slot]))

    for i in range(SLOTS):
        for copy in load(i):
            copy.start()

    barrier = pltpu.get_barrier_semaphore()
    for k in range(1, T):
        pl.semaphore_signal(barrier, inc=1, device_id={"tensor": lax.rem(t + k, T)}, device_id_type=MESH)
    for k in range(1, N):
        pl.semaphore_signal(barrier, inc=1, device_id={"dp": lax.rem(p + k, N)}, device_id_type=MESH)
    q_low = q_ref[...].astype(BF16)
    waited = T + N - 2

    def send(src, dst, a, b, axis, peer):
        return pltpu.make_async_remote_copy(
            src_ref=src, dst_ref=dst, send_sem=a, recv_sem=b,
            device_id={axis: peer}, device_id_type=MESH)

    def to_tensor(k):
        return lax.rem(t + k, T)

    def to_dp(k):
        return lax.rem(p + k, N)

    def from_dp(k):
        return lax.rem(p + (N - k), N)

    def when_owner(index, body):
        if owners == N:
            body()
        else:
            pl.when(index < owners)(body)

    def compute(c):
        def tile(i, carry):
            g, e = load(i)
            g.wait()
            e.wait()
            slot = lax.rem(i, SLOTS)
            merged = (gbuf[slot].astype(F32) + ebuf[slot].astype(F32)).astype(BF16)
            merged_ref[pl.ds(pl.multiple_of(i * rows, rows), rows), :] = merged
            part[i] = lax.dot_general(q_low, merged, NT, preferred_element_type=F32)

            @pl.when(i + SLOTS < tiles)
            def _():
                for copy in load(i + SLOTS):
                    copy.start()
            return carry
        lax.fori_loop(c * T, (c + 1) * T, tile, 0)

    def copy1(c, k):
        return send(part.at[c * T + to_tensor(k)], s1r.at[c, k - 1], s1a.at[c, k - 1], s1b.at[c, k - 1], "tensor", to_tensor(k))

    def stage1(c):
        for k in range(1, T):
            copy1(c, k).start()

    def copy2(c, k):
        piece = to_dp(k) if owners == N else jnp.minimum(to_dp(k), owners - 1)
        return send(s2s.at[c, piece], s2r.at[c, k - 1], s2a.at[c, k - 1], s2b.at[c, k - 1], "dp", to_dp(k))

    def stage2(c):
        value = part[c * T + t]
        for k in range(1, T):
            copy1(c, k).wait_recv()
            value = value + s1r[c, k - 1]
        value = value * (1.0 / N)
        for h in range(halves):
            for g in range(groups):
                s2s[c, h * groups + g] = value[g * 8:(g + 1) * 8, h * 128:(h + 1) * 128]
        for k in range(1, N):
            when_owner(to_dp(k), lambda k=k: copy2(c, k).start())

    def copy3(c, k):
        piece = full.at[c, t, p if owners == N else jnp.minimum(p, owners - 1)]
        return send(piece, piece, s3a.at[c, k - 1], s3b.at[c, k - 1], "dp", to_dp(k))

    def stage3(c):
        def body():
            value = s2s[c, p]
            for k in range(1, N):
                copy2(c, k).wait_recv()
                value = value + s2r[c, k - 1]
            full[c, t, p] = value
            for k in range(1, N):
                copy3(c, k).start()
        when_owner(p, body)

    def copy4(c, k):
        return send(full.at[c, t], full.at[c, t], s4a.at[c, k - 1], s4b.at[c, k - 1], "tensor", to_tensor(k))

    def stage4(c):
        for k in range(1, N):
            when_owner(from_dp(k), lambda k=k: copy3(c, k).wait_recv())
        for k in range(1, T):
            copy4(c, k).start()

    def chunk_left(c):
        pieces = []
        for s in range(T):
            for h in range(halves):
                pieces.append(full[c, s, h * groups:(h + 1) * groups].reshape(rank, 128))
        return jnp.concatenate(pieces, axis=1)

    length = T * rows

    def copy5(k):
        return send(s5s.at[to_dp(k)], s5r.at[k - 1], s5a.at[k - 1], s5b.at[k - 1], "dp", to_dp(k))

    def stage5(c):
        for k in range(1, T):
            copy4(c, k).wait_recv()
        left = chunk_left(c)
        left_ref[:, c * length:(c + 1) * length] = left
        both = jnp.concatenate(split(left), axis=0)
        last = c == CHUNKS - 1

        def block(b):
            where = pl.ds(pl.multiple_of(b * columns, columns), columns)
            out = jnp.dot(both, merged_ref[c * length:(c + 1) * length, where], preferred_element_type=F32)
            out = out[:rank] + out[rank:]
            if c > 0:
                out = out + acc[b]
            if not last:
                acc[b] = out
            else:
                high = rank // per
                for i in range(per):
                    s5s[b * per + i] = out[i * high:(i + 1) * high] * (1.0 / N)

        if not last or per > 1:
            def step(b, carry):
                block(b)
                return carry
            lax.fori_loop(0, blocks, step, 0)
            if last:
                for k in range(1, N):
                    copy5(k).start()
        else:
            for k in range(1, N):
                block(to_dp(k))
                copy5(k).start()
            block(p)

    compute(0)
    pl.semaphore_wait(barrier, waited)
    stage1(0)
    compute(1)
    stage1(1)
    stage2(0)
    compute(2)
    stage1(2)
    stage2(1)
    stage3(0)
    stage2(2)
    stage3(1)
    stage4(0)
    stage3(2)
    stage4(1)
    stage5(0)
    stage4(2)
    stage5(1)
    stage5(2)

    left = left_ref[...]
    gram = lax.dot_general(left, left, NT, precision=lax.Precision.HIGHEST, preferred_element_type=F32)
    state = eliminate(augmented(gram, rank), rank, range(rank // 2))

    def copy6(k):
        return send(total.at[p], total.at[p], s6a.at[k - 1], s6b.at[k - 1], "dp", to_dp(k))

    value = s5s[p]
    for k in range(1, N):
        copy5(k).wait_recv()
        value = value + s5r[k - 1]
    total[p] = value
    for k in range(1, N):
        copy6(k).start()
    work, scale = eliminate(state, rank, range(rank // 2, rank))
    inverse = (work * scale)[:, rank:2 * rank]
    basis = jnp.dot(inverse, left, precision=lax.Precision.HIGHEST, preferred_element_type=F32)
    high, low = split(basis)
    basis_ref[...] = jnp.concatenate([high, low, high], axis=0).T
    for k in range(1, N):
        copy6(k).wait_recv()
    for b in range(blocks):
        value = jnp.concatenate([total[b * per + i] for i in range(per)], axis=0)
        right_ref[:, b * columns:(b + 1) * columns] = jnp.dot(
            inverse, value, precision=lax.Precision.HIGHEST, preferred_element_type=F32)

    for c in range(CHUNKS):
        for k in range(1, T):
            copy1(c, k).wait_send()
            copy4(c, k).wait_send()
        for k in range(1, N):
            when_owner(to_dp(k), lambda k=k: copy2(c, k).wait_send())
            when_owner(p, lambda k=k: copy3(c, k).wait_send())
    for k in range(1, N):
        copy5(k).wait_send()
        copy6(k).wait_send()


def renew(basis_ref, right_ref, merged_ref, new_ref, out_ref, factor_ref):
    i = pl.program_id(0)
    rows, width = new_ref.shape

    @pl.when(i == 0)
    def _():
        right = right_ref[...]
        out_ref[...] = right
        high, low = split(right)
        factor_ref[...] = jnp.concatenate([high, high, low], axis=0)

    start = pl.multiple_of(i * rows, rows)
    step = 512
    basis = basis_ref[...]
    for b in range(width // step):
        cut = slice(b * step, (b + 1) * step)
        approx = jnp.dot(basis, factor_ref[:, cut], preferred_element_type=F32)
        new_ref[:, cut] = (merged_ref[pl.ds(start, rows), cut].astype(F32) - approx).astype(BF16)


def on_device(T, N, grads, errors, q_init):
    depth, width = grads.shape[1:]
    rank = q_init.shape[1]
    rows = depth // (CHUNKS * T)
    owners = (rank // 8) * (rows // 128)
    blocks = min(N, width // 128)
    per = N // blocks
    columns = width // blocks
    piece = (rank // per, columns)
    vmem = pl.BlockSpec(memory_space=pltpu.VMEM)
    hbm = pl.BlockSpec(memory_space=pl.ANY)
    dma = pltpu.SemaphoreType.DMA
    merged, left, basis, right = pl.pallas_call(
        functools.partial(exchange, T, N, rank),
        out_shape=(
            pltpu.VMEM((depth, width), BF16),
            jax.ShapeDtypeStruct((rank, depth), F32),
            jax.ShapeDtypeStruct((depth, 3 * rank), BF16),
            jax.ShapeDtypeStruct((rank, width), F32),
        ),
        in_specs=[hbm, hbm, vmem],
        out_specs=(vmem, vmem, vmem, vmem),
        scratch_shapes=[
            pltpu.VMEM((SLOTS, rows, width), BF16),
            pltpu.VMEM((SLOTS, rows, width), BF16),
            pltpu.VMEM((CHUNKS * T, rank, rows), F32),
            pltpu.VMEM((CHUNKS, T - 1, rank, rows), F32),
            pltpu.VMEM((CHUNKS, owners, 8, 128), F32),
            pltpu.VMEM((CHUNKS, N - 1, 8, 128), F32),
            pltpu.VMEM((CHUNKS, T, owners, 8, 128), F32),
            pltpu.VMEM((blocks, rank, columns), F32),
            pltpu.VMEM((N,) + piece, F32),
            pltpu.VMEM((N - 1,) + piece, F32),
            pltpu.VMEM((N,) + piece, F32),
            dma((SLOTS,)), dma((SLOTS,)),
            dma((CHUNKS, T - 1)), dma((CHUNKS, T - 1)),
            dma((CHUNKS, N - 1)), dma((CHUNKS, N - 1)),
            dma((CHUNKS, N - 1)), dma((CHUNKS, N - 1)),
            dma((CHUNKS, T - 1)), dma((CHUNKS, T - 1)),
            dma((N - 1,)), dma((N - 1,)),
            dma((N - 1,)), dma((N - 1,)),
        ],
        compiler_params=pltpu.CompilerParams(
            collective_id=0, has_side_effects=True, vmem_limit_bytes=40 * 2 ** 20),
    )(grads[0], errors[0], q_init.T)

    renew_rows = 256
    renewed, right_out = pl.pallas_call(
        renew,
        grid=(depth // renew_rows,),
        out_shape=(jax.ShapeDtypeStruct((depth, width), BF16), jax.ShapeDtypeStruct((rank, width), F32)),
        in_specs=[
            pl.BlockSpec((renew_rows, 3 * rank), lambda i: (i, 0)),
            pl.BlockSpec((rank, width), lambda i: (0, 0)),
            vmem,
        ],
        out_specs=(
            pl.BlockSpec((renew_rows, width), lambda i: (i, 0)),
            pl.BlockSpec((rank, width), lambda i: (0, 0)),
        ),
        scratch_shapes=[pltpu.VMEM((3 * rank, width), BF16)],
        compiler_params=pltpu.CompilerParams(vmem_limit_bytes=16 * 2 ** 20),
    )(basis, right, merged)

    share = depth // (N * T)
    position = lax.axis_index(("dp", "tensor"))
    left_out = lax.dynamic_slice_in_dim(left, position * share, share, 1).T
    return (left_out, right_out.T, renewed[None])


def solution(mesh):
    return jax.shard_map(
        functools.partial(on_device, mesh.shape["tensor"], mesh.shape["dp"]),
        mesh=mesh,
        in_specs=(P("dp", None, "tensor"), P("dp", None, "tensor"), P("tensor", None)),
        out_specs=(P(("dp", "tensor"), None), P("tensor", None), P("dp", None, "tensor")),
        check_vma=False,
    )
```
